128 devices in a mesh: mem: 4 (over z_hi, core), space: 32 (over y, x, z_lo).
Axes of the slice: x: 4, y: 4, z: 4 (z_hi: 2, z_lo: 2; z = z_hi * 2 + z_lo), core: 2. Of those that a mesh axis runs over, the one named last changes fastest.
Arguments:
- alpha: bfloat16 [64, 128, 16384], P('mem', None, 'space'), may hold values from -6 to 6
- perturbation: bfloat16 [64, 128, 16384], P('mem', None, 'space'), may hold values from -6 to 6
- vertical_loc: bfloat16 [128, 128], replicated, may hold values from -0.5 to 0.5
- tile_blocks: bfloat16 [25, 128, 128], replicated, may hold values from -0.109375 to 0.109375
- neighbours: int32 [128, 25], replicated, may hold values from 0 to 127
- tile_slot: int32 [128], replicated, may hold values from 0 to 127, each once
- member_src: int32 [4, 16], P('mem'), may hold values from 0 to 15, each once within a row
Outputs:
- increment: float32 [128, 16384], P('mem', 'space')
The draws below stay inside these ranges and needn't reach their ends.
Inputs may be any that keep to these rules, and one draw needn't show every extreme that they name: `member_src`: each row is a permutation of 0 to 15. `tile_slot`: A permutation of 0 to 127.
All inputs are finite; a program needn't handle non-finite values.
Results may differ from the reference program's by a relative error of at most 0.0041.
Values may be sent and summed in bfloat16 or wider, within the bound.
No kernel may reach another device: no remote copies, remote signals or barrier semaphores. Data moves between devices by JAX's collectives and lax.ppermute only.
A program may use at most 128 MiB of HBM per device.

```python
import jax
import jax.numpy as jnp
from jax import lax

TILE = 128
NBRS = 25
MEM_DEV = 16
LEV = 128
MEMBERS = 64
TILES = 128
COLS = 16384
N_MEM = 4


def place_ends(values, rng, least, high):
    shape = values.shape
    place = [jax.random.randint(jax.random.fold_in(rng, axis), (), 0, shape[axis]) for axis in range(len(shape))]
    values = values.at[tuple(place)].set(least)
    longest = shape.index(max(shape))
    place[longest] = (place[longest] + 1) % shape[longest]
    return values.at[tuple(place)].set(high)


def with_spikes(result, own_key, source, target, blocks, factor):
    owner, partner = [(jnp.arange(result.shape[position]) // (result.shape[position] // blocks)).reshape([-1 if axis == position else 1 for axis in range(result.ndim)]) for position in (source, target)]
    chosen = jax.random.permutation(own_key, blocks)[partner]
    strong = (owner == chosen) | (owner == (partner + blocks // 2) % blocks)
    return jnp.where(strong, factor * result, result)


def steps_of(key, extent, pieces, least, largest):
    gain = 1.0
    for position, parts in pieces:
        steps = jax.random.uniform(jax.random.fold_in(jax.random.fold_in(key, 6), position), (parts,), jnp.float32, least / len(pieces), largest / len(pieces))
        gain = gain * jnp.repeat(jnp.exp(steps), extent[position] // parts).reshape((-1,) + (1,) * (len(extent) - 1 - position))
    return gain


def gaussian(key, extent, spread, most, pieces=(), kind=jnp.bfloat16):
    gain = steps_of(key, extent, pieces, -0.22, 0.18) if pieces else 1.0
    result = jax.random.normal(key, extent, jnp.float32) * spread * gain
    return jnp.minimum(jnp.maximum(result, -most), most).astype(kind)


def heavy_noise(key, dims, width, most, shards, heavy, kind=jnp.bfloat16):
    values = width * jax.random.normal(key, dims, jnp.float32)
    if shards:
        values = values * steps_of(key, dims, shards, -0.22, 0.18)
    return jnp.clip(with_spikes(values, jax.random.fold_in(key, 3), *heavy), -most, most).astype(kind)


def setup_inputs(seed: int = 0) -> dict:
    seeds = jax.random.split(jax.random.key(seed), 8)
    alpha = gaussian(seeds[0], (MEMBERS, LEV, COLS), 1.0, 6.0, ((0, 4), (2, 32)))
    perturbation = heavy_noise(seeds[1], (MEMBERS, LEV, COLS), 1.0, 6.0, ((0, 4), (2, 32)), (0, 1, 4, 2.0))
    vertical_loc = gaussian(seeds[2], (LEV, LEV), LEV ** -0.5, 0.5)
    tile_blocks = gaussian(seeds[3], (NBRS, TILE, TILE), (NBRS * TILE) ** -0.5, 0.109375)
    neighbours = place_ends(jax.random.randint(seeds[4], (TILES, NBRS), 0, TILES), jax.random.fold_in(seeds[4], 1), 0, TILES - 1).astype(jnp.int32)
    tile_slot = jax.random.permutation(seeds[5], TILES).astype(jnp.int32)
    member_src = jax.vmap(lambda own: jax.random.permutation(own, MEM_DEV))(jax.random.split(seeds[6], N_MEM)).reshape((N_MEM, MEM_DEV)).astype(jnp.int32)
    return {"alpha": alpha, "perturbation": perturbation, "vertical_loc": vertical_loc, "tile_blocks": tile_blocks, "neighbours": neighbours, "tile_slot": tile_slot, "member_src": member_src}


def localize_field(level_field, index_table, tile_blocks):
    row_block = level_field.astype(jnp.float32).reshape(LEV, TILES, TILE)
    blocks_f = tile_blocks.astype(jnp.float32)

    def add_term(total, scan_item):
        slot_cols, weights = scan_item
        picked = jnp.take(row_block, slot_cols, axis=1)
        return (total + jnp.einsum('rtc,cd->rtd', picked, weights), None)
    start = jnp.zeros((LEV, TILES, TILE), jnp.float32)
    total, _ = lax.scan(add_term, start, (index_table.T, blocks_f))
    return total.reshape(LEV, COLS).astype(jnp.bfloat16)

def reference(alpha, perturbation, vertical_loc, tile_blocks, neighbours, tile_slot, member_src):
    slot_of_tile = jnp.zeros((TILES,), jnp.int32).at[tile_slot].set(jnp.arange(TILES, dtype=jnp.int32))
    index_table = slot_of_tile[neighbours[tile_slot]].astype(jnp.int32)
    source_rows = (member_src + jnp.arange(N_MEM, dtype=jnp.int32)[:, None] * MEM_DEV).reshape(-1).astype(jnp.int32)

    def add_member(total, scan_item):
        member_field, source_row = scan_item
        vert = jnp.dot(vertical_loc, member_field, preferred_element_type=jnp.float32).astype(jnp.bfloat16)
        localized = localize_field(vert, index_table, tile_blocks)
        selected = lax.dynamic_index_in_dim(perturbation, source_row, 0, keepdims=False)
        return (total + selected.astype(jnp.float32) * localized.astype(jnp.float32), None)
    start = jnp.zeros((LEV, COLS), jnp.float32)
    total, _ = lax.scan(add_member, start, (alpha, source_rows))
    return total / jnp.sqrt(jnp.float32(MEMBERS - 1))
```

```python
import jax
import jax.numpy as jnp
from jax import lax
from jax.experimental import pallas as pl
from jax.experimental.pallas import tpu as pltpu
from jax.sharding import PartitionSpec as P

MIB = 1024 * 1024
LANES = 128


def put_member(rows_ref, m, members, field):
    levels, width = field.shape
    for q in range(width // LANES):
        rows_ref[q, pl.ds(m, levels, stride=members), :] = field[:, q * LANES : (q + 1) * LANES]


def write_out(rows_ref, out_ref):
    levels, members, width = out_ref.shape
    for q in range(width // LANES):
        out_ref[:, :, q * LANES : (q + 1) * LANES] = (
            rows_ref[q].astype(jnp.bfloat16).reshape(levels, members, LANES)
        )


def vertical_kernel(loc_ref, alpha_ref, out_ref, rows_ref):
    members = alpha_ref.shape[0]
    for m in range(members):
        field = jnp.dot(loc_ref[...], alpha_ref[m], preferred_element_type=jnp.float32)
        put_member(rows_ref, m, members, field)
    write_out(rows_ref, out_ref)


def vertical(alpha, vertical_loc, steps=2):
    members, levels, cols = alpha.shape
    width = cols // steps
    return pl.pallas_call(
        vertical_kernel,
        grid=(steps,),
        in_specs=[
            pl.BlockSpec((levels, levels), lambda c: (0, 0)),
            pl.BlockSpec((members, levels, width), lambda c: (0, 0, c)),
        ],
        out_specs=pl.BlockSpec((levels, members, width), lambda c: (0, 0, c)),
        out_shape=jax.ShapeDtypeStruct((levels, members, cols), jnp.bfloat16),
        scratch_shapes=[pltpu.VMEM((width // LANES, levels * members, LANES), jnp.float32)],
        compiler_params=pltpu.CompilerParams(vmem_limit_bytes=32 * MIB),
        cost_estimate=pl.CostEstimate(
            flops=2 * members * levels * levels * cols,
            bytes_accessed=4 * members * levels * cols,
            transcendentals=0,
        ),
        name="vertical",
    )(vertical_loc, alpha)


def select_kernel(src_ref, pert_ref, out_ref, rows_ref):
    members = pert_ref.shape[0]
    for m in range(members):
        put_member(rows_ref, m, members, pert_ref[src_ref[m]].astype(jnp.float32))
    write_out(rows_ref, out_ref)


def select(perturbation, member_src, steps=2):
    members, levels, cols = perturbation.shape
    width = cols // steps
    return pl.pallas_call(
        select_kernel,
        grid=(steps,),
        in_specs=[
            pl.BlockSpec(memory_space=pltpu.SMEM),
            pl.BlockSpec((members, levels, width), lambda c: (0, 0, c)),
        ],
        out_specs=pl.BlockSpec((levels, members, width), lambda c: (0, 0, c)),
        out_shape=jax.ShapeDtypeStruct((levels, members, cols), jnp.bfloat16),
        scratch_shapes=[pltpu.VMEM((width // LANES, levels * members, LANES), jnp.float32)],
        compiler_params=pltpu.CompilerParams(vmem_limit_bytes=32 * MIB),
        cost_estimate=pl.CostEstimate(
            flops=0, bytes_accessed=4 * members * levels * cols, transcendentals=0
        ),
        name="select",
    )(member_src, perturbation)


def localize_kernel(neigh_ref, slot_ref, vert_ref, blocks_ref, out_ref, slot_of_ref, tiles_ref, picked_ref):
    groups, senders, members, cols = vert_ref.shape
    tile_count, rows, tile = tiles_ref.shape
    nbrs = blocks_ref.shape[0] // tile
    per_sender = cols // tile
    here = out_ref.shape[1]
    block = pl.program_id(0)

    @pl.when(block == 0)
    def _():
        def number(s, carry):
            slot_of_ref[slot_ref[s]] = s
            return carry

        lax.fori_loop(0, tile_count, number, 0)

        def stack(sender, carry):
            for g in range(groups):
                for q in range(per_sender):
                    tiles_ref[sender * per_sender + q, pl.ds(g * members, members), :] = vert_ref[
                        g, sender, :, pl.ds(q * tile, tile)
                    ]
            return carry

        lax.fori_loop(0, senders, stack, 0)

    def pick(i, carry):
        first = slot_ref[block * here * per_sender + i] * nbrs
        for k in range(nbrs):
            picked_ref[pl.ds(pl.multiple_of(i * rows, rows), rows), pl.ds(k * tile, tile)] = tiles_ref[
                slot_of_ref[neigh_ref[first + k]]
            ]
        return carry

    lax.fori_loop(0, here * per_sender, pick, 0)
    result = jnp.dot(picked_ref[...], blocks_ref[...], preferred_element_type=jnp.float32).astype(
        jnp.bfloat16
    )
    for s in range(here):
        for q in range(per_sender):
            for g in range(groups):
                start = (s * per_sender + q) * rows + g * members
                out_ref[g, s, :, q * tile : (q + 1) * tile] = result[start : start + members]


def localize(vert, neighbours, tile_slot, tile_blocks, here=4):
    groups, senders, members, cols = vert.shape
    nbrs, tile, _ = tile_blocks.shape
    tile_count = tile_slot.shape[0]
    rows = groups * members
    return pl.pallas_call(
        localize_kernel,
        grid=(senders // here,),
        in_specs=[
            pl.BlockSpec(memory_space=pltpu.SMEM),
            pl.BlockSpec(memory_space=pltpu.SMEM),
            pl.BlockSpec((groups, senders, members, cols), lambda b: (0, 0, 0, 0)),
            pl.BlockSpec((nbrs * tile, tile), lambda b: (0, 0)),
        ],
        out_specs=pl.BlockSpec((groups, here, members, cols), lambda b: (0, b, 0, 0)),
        out_shape=jax.ShapeDtypeStruct(vert.shape, jnp.bfloat16),
        scratch_shapes=[
            pltpu.SMEM((tile_count,), jnp.int32),
            pltpu.VMEM((tile_count, rows, tile), jnp.bfloat16),
            pltpu.VMEM((here * (cols // tile) * rows, nbrs * tile), jnp.bfloat16),
        ],
        compiler_params=pltpu.CompilerParams(vmem_limit_bytes=40 * MIB),
        cost_estimate=pl.CostEstimate(
            flops=2 * rows * tile_count * nbrs * tile * tile,
            bytes_accessed=4 * rows * tile_count * tile,
            transcendentals=0,
        ),
        name="localize",
    )(neighbours.reshape(-1), tile_slot, vert, tile_blocks.reshape(nbrs * tile, tile))


def weigh_kernel(loc_ref, pert_ref, out_ref, *, scale):
    groups, here, members, cols = loc_ref.shape
    for s in range(here):
        total = jnp.zeros((members, cols), jnp.float32)
        for g in range(groups):
            total = total + loc_ref[g, s].astype(jnp.float32) * pert_ref[g, s].astype(jnp.float32)
        out_ref[s] = jnp.sum(total, axis=0, keepdims=True) * scale


def weigh(localized, selected, scale, here=8):
    groups, senders, members, cols = localized.shape
    spec = pl.BlockSpec((groups, here, members, cols), lambda b: (0, b, 0, 0))
    return pl.pallas_call(
        lambda *refs: weigh_kernel(*refs, scale=scale),
        grid=(senders // here,),
        in_specs=[spec, spec],
        out_specs=pl.BlockSpec((here, 1, cols), lambda b: (b, 0, 0)),
        out_shape=jax.ShapeDtypeStruct((senders, 1, cols), jnp.float32),
        compiler_params=pltpu.CompilerParams(vmem_limit_bytes=32 * MIB),
        cost_estimate=pl.CostEstimate(
            flops=2 * groups * senders * members * cols,
            bytes_accessed=4 * groups * senders * members * cols,
            transcendentals=0,
        ),
        name="weigh",
    )(localized, selected)


def on_device(alpha, perturbation, vertical_loc, tile_blocks, neighbours, tile_slot, member_src):
    groups, senders = lax.axis_size("mem"), lax.axis_size("space")
    members, levels, cols = alpha.shape
    everyone = ("mem", "space")
    scale = 1.0 / float(groups * members - 1) ** 0.5

    def to_level_owner(fields):
        return lax.all_to_all(fields, everyone, 0, 0, tiled=True).reshape(
            groups, senders, members, cols
        )

    vert = to_level_owner(vertical(alpha, vertical_loc))
    selected = to_level_owner(select(perturbation, member_src.reshape(-1)))
    localized = localize(vert, neighbours, tile_slot, tile_blocks)
    increment = weigh(localized, selected, scale)
    increment = lax.all_to_all(increment, "space", 0, 0, tiled=True)
    return increment.reshape(senders, cols)


def solution(mesh):
    return jax.shard_map(
        on_device,
        mesh=mesh,
        in_specs=(
            P("mem", None, "space"),
            P("mem", None, "space"),
            P(),
            P(),
            P(),
            P(),
            P("mem", None),
        ),
        out_specs=P("mem", "space"),
        check_vma=False,
    )
```

```python
import jax
import jax.numpy as jnp
from jax import lax
from jax.experimental import pallas as pl
from jax.experimental.pallas import tpu as pltpu
from jax.sharding import PartitionSpec as P

MIB = 1024 * 1024


def by_level(fields, out_ref):
    owners, own, _, _ = out_ref.shape
    ordered = jnp.swapaxes(fields, 0, 1).astype(jnp.bfloat16)
    for a in range(own):
        out_ref[:, a] = ordered[a * owners : (a + 1) * owners]


def vertical_kernel(loc_ref, alpha_ref, out_ref):
    fields = [
        jnp.dot(loc_ref[...], alpha_ref[m], preferred_element_type=jnp.float32)
        for m in range(alpha_ref.shape[0])
    ]
    by_level(jnp.stack(fields), out_ref)


def vertical(alpha, vertical_loc, owners, steps=2):
    members, levels, cols = alpha.shape
    width = cols // steps
    own = levels // owners
    return pl.pallas_call(
        vertical_kernel,
        grid=(steps,),
        in_specs=[
            pl.BlockSpec((levels, levels), lambda c: (0, 0)),
            pl.BlockSpec((members, levels, width), lambda c: (0, 0, c)),
        ],
        out_specs=pl.BlockSpec((owners, own, members, width), lambda c: (0, 0, 0, c)),
        out_shape=jax.ShapeDtypeStruct((owners, own, members, cols), jnp.bfloat16),
        compiler_params=pltpu.CompilerParams(vmem_limit_bytes=60 * MIB),
        cost_estimate=pl.CostEstimate(
            flops=2 * members * levels * levels * cols,
            bytes_accessed=4 * members * levels * cols,
            transcendentals=0,
        ),
        name="vertical",
    )(vertical_loc, alpha)


def select_kernel(src_ref, pert_ref, out_ref):
    members = pert_ref.shape[0]
    by_level(
        jnp.stack([pert_ref[src_ref[m]].astype(jnp.float32) for m in range(members)]), out_ref
    )


def select(perturbation, member_src, owners, steps=2):
    members, levels, cols = perturbation.shape
    width = cols // steps
    own = levels // owners
    return pl.pallas_call(
        select_kernel,
        grid=(steps,),
        in_specs=[
            pl.BlockSpec(memory_space=pltpu.SMEM),
            pl.BlockSpec((members, levels, width), lambda c: (0, 0, c)),
        ],
        out_specs=pl.BlockSpec((owners, own, members, width), lambda c: (0, 0, 0, c)),
        out_shape=jax.ShapeDtypeStruct((owners, own, members, cols), jnp.bfloat16),
        compiler_params=pltpu.CompilerParams(vmem_limit_bytes=32 * MIB),
        cost_estimate=pl.CostEstimate(
            flops=0, bytes_accessed=4 * members * levels * cols, transcendentals=0
        ),
        name="select",
    )(member_src, perturbation)


def localize_kernel(neigh_ref, slot_ref, vert_ref, blocks_ref, out_ref, slot_of_ref, tiles_ref):
    groups, senders, members, cols = vert_ref.shape
    tile_count, rows, tile = tiles_ref.shape
    nbrs = blocks_ref.shape[0] // tile
    per_sender = cols // tile
    here = out_ref.shape[1]
    block = pl.program_id(0)

    @pl.when(block == 0)
    def _():
        def number(s, carry):
            slot_of_ref[slot_ref[s]] = s
            return carry

        lax.fori_loop(0, tile_count, number, 0, unroll=8)

        def split(sender, carry):
            for g in range(groups):
                for q in range(per_sender):
                    tiles_ref[sender * per_sender + q, g * members : (g + 1) * members] = vert_ref[
                        g, sender, :, q * tile : (q + 1) * tile
                    ]
            return carry

        lax.fori_loop(0, senders, split, 0, unroll=2)

    count = here * per_sender
    firsts = [slot_ref[block * count + i] * nbrs for i in range(count)]

    def picked(i, k):
        return tiles_ref[slot_of_ref[neigh_ref[firsts[i] + k]]]

    total = None
    for k in range(0, nbrs, 2):
        both = range(k, min(k + 2, nbrs))
        left = jnp.concatenate(
            [jnp.concatenate([picked(i, b) for b in both], axis=1) for i in range(count)], axis=0
        )
        term = jnp.dot(
            left,
            blocks_ref[k * tile : (k + len(both)) * tile, :],
            preferred_element_type=jnp.float32,
        )
        total = term if total is None else total + term
    total = total.astype(jnp.bfloat16)
    for i in range(count):
        s, q = divmod(i, per_sender)
        for g in range(groups):
            start = i * rows + g * members
            out_ref[g, s, :, q * tile : (q + 1) * tile] = total[start : start + members]


def localize(vert, neighbours, tile_slot, tile_blocks, here=4):
    groups, senders, members, cols = vert.shape
    rows = groups * members
    nbrs, tile, _ = tile_blocks.shape
    tile_count = tile_slot.shape[0]
    return pl.pallas_call(
        localize_kernel,
        grid=(senders // here,),
        in_specs=[
            pl.BlockSpec(memory_space=pltpu.SMEM),
            pl.BlockSpec(memory_space=pltpu.SMEM),
            pl.BlockSpec((groups, senders, members, cols), lambda b: (0, 0, 0, 0)),
            pl.BlockSpec((nbrs * tile, tile), lambda b: (0, 0)),
        ],
        out_specs=pl.BlockSpec((groups, here, members, cols), lambda b: (0, b, 0, 0)),
        out_shape=jax.ShapeDtypeStruct(vert.shape, jnp.bfloat16),
        scratch_shapes=[
            pltpu.SMEM((tile_count,), jnp.int32),
            pltpu.VMEM((tile_count, rows, tile), jnp.bfloat16),
        ],
        compiler_params=pltpu.CompilerParams(vmem_limit_bytes=24 * MIB),
        cost_estimate=pl.CostEstimate(
            flops=2 * rows * tile_count * nbrs * tile * tile,
            bytes_accessed=4 * rows * tile_count * tile,
            transcendentals=0,
        ),
        name="localize",
    )(neighbours.reshape(-1), tile_slot, vert, tile_blocks.reshape(nbrs * tile, tile))


def weigh_kernel(loc_ref, pert_ref, out_ref, *, scale):
    groups, here, members, cols = loc_ref.shape
    for s in range(here):
        total = jnp.zeros((members, cols), jnp.float32)
        for g in range(groups):
            total = total + loc_ref[g, s].astype(jnp.float32) * pert_ref[g, s].astype(jnp.float32)
        out_ref[s] = jnp.sum(total, axis=0, keepdims=True) * scale


def weigh(localized, selected, scale, here=8):
    groups, senders, members, cols = localized.shape
    spec = pl.BlockSpec((groups, here, members, cols), lambda b: (0, b, 0, 0))
    return pl.pallas_call(
        lambda *refs: weigh_kernel(*refs, scale=scale),
        grid=(senders // here,),
        in_specs=[spec, spec],
        out_specs=pl.BlockSpec((here, 1, cols), lambda b: (b, 0, 0)),
        out_shape=jax.ShapeDtypeStruct((senders, 1, cols), jnp.float32),
        compiler_params=pltpu.CompilerParams(vmem_limit_bytes=32 * MIB),
        cost_estimate=pl.CostEstimate(
            flops=2 * groups * senders * members * cols,
            bytes_accessed=4 * groups * senders * members * cols,
            transcendentals=0,
        ),
        name="weigh",
    )(localized, selected)


def on_device(alpha, perturbation, vertical_loc, tile_blocks, neighbours, tile_slot, member_src):
    groups, senders = lax.axis_size("mem"), lax.axis_size("space")
    members, levels, cols = alpha.shape
    own = 1
    everyone = ("mem", "space")
    owners = groups * senders
    scale = 1.0 / float(groups * members - 1) ** 0.5

    def to_level_owner(fields):
        fields = lax.all_to_all(fields.reshape(owners, members, cols), everyone, 0, 0, tiled=True)
        return fields.reshape(groups, senders, members, cols)

    vert = to_level_owner(vertical(alpha, vertical_loc, owners))
    selected = to_level_owner(select(perturbation, member_src.reshape(-1), owners))
    localized = localize(vert, neighbours, tile_slot, tile_blocks)
    increment = weigh(localized, selected, scale)
    increment = lax.all_to_all(increment, "space", 0, 0, tiled=True)
    return increment.reshape(senders, cols)


def solution(mesh):
    return jax.shard_map(
        on_device,
        mesh=mesh,
        in_specs=(
            P("mem", None, "space"),
            P("mem", None, "space"),
            P(),
            P(),
            P(),
            P(),
            P("mem", None),
        ),
        out_specs=P("mem", "space"),
        check_vma=False,
    )
```

```python
import jax
import jax.numpy as jnp
from jax import lax
from jax.experimental import pallas as pl
from jax.experimental.pallas import tpu as pltpu
from jax.sharding import PartitionSpec as P

MIB = 1024 * 1024


def by_level(fields, out_ref):
    owners, own, _, _ = out_ref.shape
    ordered = jnp.swapaxes(fields, 0, 1).astype(jnp.bfloat16)
    for a in range(own):
        out_ref[:, a] = ordered[a * owners : (a + 1) * owners]


def vertical_kernel(loc_ref, alpha_ref, out_ref):
    fields = [
        jnp.dot(loc_ref[...], alpha_ref[m], preferred_element_type=jnp.float32)
        for m in range(alpha_ref.shape[0])
    ]
    by_level(jnp.stack(fields), out_ref)


def vertical(alpha, vertical_loc, owners, steps=2):
    members, levels, cols = alpha.shape
    width = cols // steps
    own = levels // owners
    return pl.pallas_call(
        vertical_kernel,
        grid=(steps,),
        in_specs=[
            pl.BlockSpec((levels, levels), lambda c: (0, 0)),
            pl.BlockSpec((members, levels, width), lambda c: (0, 0, c)),
        ],
        out_specs=pl.BlockSpec((owners, own, members, width), lambda c: (0, 0, 0, c)),
        out_shape=jax.ShapeDtypeStruct((owners, own, members, cols), jnp.bfloat16),
        compiler_params=pltpu.CompilerParams(vmem_limit_bytes=60 * MIB),
        cost_estimate=pl.CostEstimate(
            flops=2 * members * levels * levels * cols,
            bytes_accessed=4 * members * levels * cols,
            transcendentals=0,
        ),
        name="vertical",
    )(vertical_loc, alpha)


def select_kernel(src_ref, pert_ref, out_ref):
    members = pert_ref.shape[0]
    by_level(
        jnp.stack([pert_ref[src_ref[m]].astype(jnp.float32) for m in range(members)]), out_ref
    )


def select(perturbation, member_src, owners, steps=2):
    members, levels, cols = perturbation.shape
    width = cols // steps
    own = levels // owners
    return pl.pallas_call(
        select_kernel,
        grid=(steps,),
        in_specs=[
            pl.BlockSpec(memory_space=pltpu.SMEM),
            pl.BlockSpec((members, levels, width), lambda c: (0, 0, c)),
        ],
        out_specs=pl.BlockSpec((owners, own, members, width), lambda c: (0, 0, 0, c)),
        out_shape=jax.ShapeDtypeStruct((owners, own, members, cols), jnp.bfloat16),
        compiler_params=pltpu.CompilerParams(vmem_limit_bytes=32 * MIB),
        cost_estimate=pl.CostEstimate(
            flops=0, bytes_accessed=4 * members * levels * cols, transcendentals=0
        ),
        name="select",
    )(member_src, perturbation)


def localize_kernel(neigh_ref, slot_ref, vert_ref, blocks_ref, out_ref, slot_of_ref, tiles_ref):
    groups, senders, members, cols = vert_ref.shape
    tile_count, rows, tile = tiles_ref.shape
    nbrs = blocks_ref.shape[0] // tile
    per_sender = cols // tile
    here = out_ref.shape[1]
    block = pl.program_id(0)

    @pl.when(block == 0)
    def _():
        def number(s, carry):
            slot_of_ref[slot_ref[s]] = s
            return carry

        lax.fori_loop(0, tile_count, number, 0, unroll=8)

        def split(sender, carry):
            for g in range(groups):
                for q in range(per_sender):
                    tiles_ref[sender * per_sender + q, g * members : (g + 1) * members] = vert_ref[
                        g, sender, :, q * tile : (q + 1) * tile
                    ]
            return carry

        lax.fori_loop(0, senders, split, 0, unroll=2)

    count = here * per_sender
    firsts = [slot_ref[block * count + i] * nbrs for i in range(count)]

    def picked(i, k):
        return tiles_ref[slot_of_ref[neigh_ref[firsts[i] + k]]]

    total = None
    for k in range(0, nbrs, 2):
        both = range(k, min(k + 2, nbrs))
        left = jnp.concatenate(
            [jnp.concatenate([picked(i, b) for b in both], axis=1) for i in range(count)], axis=0
        )
        term = jnp.dot(
            left,
            blocks_ref[k * tile : (k + len(both)) * tile, :],
            preferred_element_type=jnp.float32,
        )
        total = term if total is None else total + term
    total = total.astype(jnp.bfloat16)
    for i in range(count):
        s, q = divmod(i, per_sender)
        for g in range(groups):
            start = i * rows + g * members
            out_ref[g, s, :, q * tile : (q + 1) * tile] = total[start : start + members]


def localize(vert, neighbours, tile_slot, tile_blocks, here=4):
    groups, senders, members, cols = vert.shape
    rows = groups * members
    nbrs, tile, _ = tile_blocks.shape
    tile_count = tile_slot.shape[0]
    return pl.pallas_call(
        localize_kernel,
        grid=(senders // here,),
        in_specs=[
            pl.BlockSpec(memory_space=pltpu.SMEM),
            pl.BlockSpec(memory_space=pltpu.SMEM),
            pl.BlockSpec((groups, senders, members, cols), lambda b: (0, 0, 0, 0)),
            pl.BlockSpec((nbrs * tile, tile), lambda b: (0, 0)),
        ],
        out_specs=pl.BlockSpec((groups, here, members, cols), lambda b: (0, b, 0, 0)),
        out_shape=jax.ShapeDtypeStruct(vert.shape, jnp.bfloat16),
        scratch_shapes=[
            pltpu.SMEM((tile_count,), jnp.int32),
            pltpu.VMEM((tile_count, rows, tile), jnp.bfloat16),
        ],
        compiler_params=pltpu.CompilerParams(vmem_limit_bytes=24 * MIB),
        cost_estimate=pl.CostEstimate(
            flops=2 * rows * tile_count * nbrs * tile * tile,
            bytes_accessed=4 * rows * tile_count * tile,
            transcendentals=0,
        ),
        name="localize",
    )(neighbours.reshape(-1), tile_slot, vert, tile_blocks.reshape(nbrs * tile, tile))


def weigh_kernel(loc_hbm, pert_ref, out_ref, loc_ref, sems, *, scale):
    parts, groups, here, members, cols = loc_ref.shape
    fetches = [
        pltpu.make_async_copy(loc_hbm.at[:, pl.ds(b * here, here)], loc_ref.at[b], sems.at[b])
        for b in range(parts)
    ]
    for fetch in fetches:
        fetch.start()
    for b in range(parts):
        fetches[b].wait()
        for s in range(here):
            total = jnp.zeros((members, cols), jnp.float32)
            for g in range(groups):
                total = total + loc_ref[b, g, s].astype(jnp.float32) * pert_ref[
                    g, b * here + s
                ].astype(jnp.float32)
            out_ref[b * here + s] = jnp.sum(total, axis=0, keepdims=True) * scale


def weigh(localized, selected, scale, parts=4):
    groups, senders, members, cols = localized.shape
    return pl.pallas_call(
        lambda *refs: weigh_kernel(*refs, scale=scale),
        in_specs=[
            pl.BlockSpec(memory_space=pltpu.HBM),
            pl.BlockSpec(memory_space=pltpu.VMEM),
        ],
        out_specs=pl.BlockSpec(memory_space=pltpu.VMEM),
        out_shape=jax.ShapeDtypeStruct((senders, 1, cols), jnp.float32),
        scratch_shapes=[
            pltpu.VMEM((parts, groups, senders // parts, members, cols), jnp.bfloat16),
            pltpu.SemaphoreType.DMA((parts,)),
        ],
        compiler_params=pltpu.CompilerParams(vmem_limit_bytes=24 * MIB),
        cost_estimate=pl.CostEstimate(
            flops=2 * groups * senders * members * cols,
            bytes_accessed=4 * groups * senders * members * cols,
            transcendentals=0,
        ),
        name="weigh",
    )(localized, selected)


def on_device(alpha, perturbation, vertical_loc, tile_blocks, neighbours, tile_slot, member_src):
    groups, senders = lax.axis_size("mem"), lax.axis_size("space")
    members, levels, cols = alpha.shape
    own = 1
    everyone = ("mem", "space")
    owners = groups * senders
    scale = 1.0 / float(groups * members - 1) ** 0.5

    def to_level_owner(fields):
        fields = lax.all_to_all(fields.reshape(owners, members, cols), everyone, 0, 0, tiled=True)
        return fields.reshape(groups, senders, members, cols)

    vert = to_level_owner(vertical(alpha, vertical_loc, owners))
    selected = to_level_owner(select(perturbation, member_src.reshape(-1), owners))
    localized = localize(vert, neighbours, tile_slot, tile_blocks)
    increment = weigh(localized, selected, scale)
    increment = lax.all_to_all(increment, "space", 0, 0, tiled=True)
    return increment.reshape(senders, cols)


def solution(mesh):
    return jax.shard_map(
        on_device,
        mesh=mesh,
        in_specs=(
            P("mem", None, "space"),
            P("mem", None, "space"),
            P(),
            P(),
            P(),
            P(),
            P("mem", None),
        ),
        out_specs=P("mem", "space"),
        check_vma=False,
    )
```

```python
import jax
import jax.numpy as jnp
from jax import lax
from jax.experimental import pallas as pl
from jax.experimental.pallas import tpu as pltpu
from jax.sharding import PartitionSpec as P

MIB = 1024 * 1024


def by_level(fields, out_ref):
    owners, own, _, _ = out_ref.shape
    ordered = jnp.swapaxes(fields, 0, 1).astype(jnp.bfloat16)
    for a in range(own):
        out_ref[:, a] = ordered[a * owners : (a + 1) * owners]


def vertical_kernel(loc_ref, alpha_ref, out_ref):
    fields = [
        jnp.dot(loc_ref[...], alpha_ref[m], preferred_element_type=jnp.float32)
        for m in range(alpha_ref.shape[0])
    ]
    by_level(jnp.stack(fields), out_ref)


def vertical(alpha, vertical_loc, owners, steps=2):
    members, levels, cols = alpha.shape
    width = cols // steps
    own = levels // owners
    return pl.pallas_call(
        vertical_kernel,
        grid=(steps,),
        in_specs=[
            pl.BlockSpec((levels, levels), lambda c: (0, 0)),
            pl.BlockSpec((members, levels, width), lambda c: (0, 0, c)),
        ],
        out_specs=pl.BlockSpec((owners, own, members, width), lambda c: (0, 0, 0, c)),
        out_shape=jax.ShapeDtypeStruct((owners, own, members, cols), jnp.bfloat16),
        compiler_params=pltpu.CompilerParams(vmem_limit_bytes=60 * MIB),
        cost_estimate=pl.CostEstimate(
            flops=2 * members * levels * levels * cols,
            bytes_accessed=4 * members * levels * cols,
            transcendentals=0,
        ),
        name="vertical",
    )(vertical_loc, alpha)


def select_kernel(src_ref, pert_ref, out_ref):
    members = pert_ref.shape[0]
    by_level(
        jnp.stack([pert_ref[src_ref[m]].astype(jnp.float32) for m in range(members)]), out_ref
    )


def select(perturbation, member_src, owners, steps=2):
    members, levels, cols = perturbation.shape
    width = cols // steps
    own = levels // owners
    return pl.pallas_call(
        select_kernel,
        grid=(steps,),
        in_specs=[
            pl.BlockSpec(memory_space=pltpu.SMEM),
            pl.BlockSpec((members, levels, width), lambda c: (0, 0, c)),
        ],
        out_specs=pl.BlockSpec((owners, own, members, width), lambda c: (0, 0, 0, c)),
        out_shape=jax.ShapeDtypeStruct((owners, own, members, cols), jnp.bfloat16),
        compiler_params=pltpu.CompilerParams(vmem_limit_bytes=32 * MIB),
        cost_estimate=pl.CostEstimate(
            flops=0, bytes_accessed=4 * members * levels * cols, transcendentals=0
        ),
        name="select",
    )(member_src, perturbation)


def localize_kernel(neigh_ref, slot_ref, vert_ref, blocks_ref, out_ref, slot_of_ref, tiles_ref):
    groups, senders, members, cols = vert_ref.shape
    tile_count, rows, tile = tiles_ref.shape
    nbrs = blocks_ref.shape[0] // tile
    per_sender = cols // tile
    here = out_ref.shape[1]
    block = pl.program_id(0)

    @pl.when(block == 0)
    def _():
        def number(s, carry):
            slot_of_ref[slot_ref[s]] = s
            return carry

        lax.fori_loop(0, tile_count, number, 0, unroll=8)

        def split(sender, carry):
            for g in range(groups):
                for q in range(per_sender):
                    tiles_ref[sender * per_sender + q, g * members : (g + 1) * members] = vert_ref[
                        g, sender, :, q * tile : (q + 1) * tile
                    ]
            return carry

        lax.fori_loop(0, senders, split, 0, unroll=2)

    count = here * per_sender
    firsts = [slot_ref[block * count + i] * nbrs for i in range(count)]

    def picked(i, k):
        return tiles_ref[slot_of_ref[neigh_ref[firsts[i] + k]]]

    total = None
    for k in range(0, nbrs, 2):
        both = range(k, min(k + 2, nbrs))
        left = jnp.concatenate(
            [jnp.concatenate([picked(i, b) for b in both], axis=1) for i in range(count)], axis=0
        )
        term = jnp.dot(
            left,
            blocks_ref[k * tile : (k + len(both)) * tile, :],
            preferred_element_type=jnp.float32,
        )
        total = term if total is None else total + term
    total = total.astype(jnp.bfloat16)
    for i in range(count):
        s, q = divmod(i, per_sender)
        for g in range(groups):
            start = i * rows + g * members
            out_ref[g, s, :, q * tile : (q + 1) * tile] = total[start : start + members]


def localize(vert, neighbours, tile_slot, tile_blocks, here=4):
    groups, senders, members, cols = vert.shape
    rows = groups * members
    nbrs, tile, _ = tile_blocks.shape
    tile_count = tile_slot.shape[0]
    return pl.pallas_call(
        localize_kernel,
        grid=(senders // here,),
        in_specs=[
            pl.BlockSpec(memory_space=pltpu.SMEM),
            pl.BlockSpec(memory_space=pltpu.SMEM),
            pl.BlockSpec((groups, senders, members, cols), lambda b: (0, 0, 0, 0)),
            pl.BlockSpec((nbrs * tile, tile), lambda b: (0, 0)),
        ],
        out_specs=pl.BlockSpec((groups, here, members, cols), lambda b: (0, b, 0, 0)),
        out_shape=jax.ShapeDtypeStruct(vert.shape, jnp.bfloat16),
        scratch_shapes=[
            pltpu.SMEM((tile_count,), jnp.int32),
            pltpu.VMEM((tile_count, rows, tile), jnp.bfloat16),
        ],
        compiler_params=pltpu.CompilerParams(vmem_limit_bytes=24 * MIB),
        cost_estimate=pl.CostEstimate(
            flops=2 * rows * tile_count * nbrs * tile * tile,
            bytes_accessed=4 * rows * tile_count * tile,
            transcendentals=0,
        ),
        name="localize",
    )(neighbours.reshape(-1), tile_slot, vert, tile_blocks.reshape(nbrs * tile, tile))


def weigh_kernel(loc_hbm, pert_ref, out_ref, loc_ref, sems, *, scale):
    parts, groups, here, members, cols = loc_ref.shape
    fetches = [
        pltpu.make_async_copy(loc_hbm.at[:, pl.ds(b * here, here)], loc_ref.at[b], sems.at[b])
        for b in range(parts)
    ]
    for fetch in fetches:
        fetch.start()
    for b in range(parts):
        fetches[b].wait()
        for s in range(here):
            total = jnp.zeros((members, cols), jnp.float32)
            for g in range(groups):
                total = total + loc_ref[b, g, s].astype(jnp.float32) * pert_ref[
                    g, b * here + s
                ].astype(jnp.float32)
            out_ref[b * here + s] = jnp.sum(total, axis=0, keepdims=True) * scale


def weigh(localized, selected, scale, parts=4):
    groups, senders, members, cols = localized.shape
    return pl.pallas_call(
        lambda *refs: weigh_kernel(*refs, scale=scale),
        in_specs=[
            pl.BlockSpec(memory_space=pltpu.HBM),
            pl.BlockSpec(memory_space=pltpu.VMEM),
        ],
        out_specs=pl.BlockSpec(memory_space=pltpu.VMEM),
        out_shape=jax.ShapeDtypeStruct((senders, 1, cols), jnp.float32),
        scratch_shapes=[
            pltpu.VMEM((parts, groups, senders // parts, members, cols), jnp.bfloat16),
            pltpu.SemaphoreType.DMA((parts,)),
        ],
        compiler_params=pltpu.CompilerParams(vmem_limit_bytes=24 * MIB),
        cost_estimate=pl.CostEstimate(
            flops=2 * groups * senders * members * cols,
            bytes_accessed=4 * groups * senders * members * cols,
            transcendentals=0,
        ),
        name="weigh",
    )(localized, selected)


def on_device(alpha, perturbation, vertical_loc, tile_blocks, neighbours, tile_slot, member_src):
    groups, senders = lax.axis_size("mem"), lax.axis_size("space")
    members, levels, cols = alpha.shape
    own = 1
    everyone = ("mem", "space")
    owners = groups * senders
    scale = 1.0 / float(groups * members - 1) ** 0.5

    def to_level_owner(fields):
        fields = lax.all_to_all(fields.reshape(owners, members, cols), everyone, 0, 0, tiled=True)
        return fields.reshape(groups, senders, members, cols)

    vert, perturbation = lax.optimization_barrier(
        (vertical(alpha, vertical_loc, owners), perturbation)
    )
    vert = to_level_owner(vert)
    selected = to_level_owner(select(perturbation, member_src.reshape(-1), owners))
    localized = localize(vert, neighbours, tile_slot, tile_blocks)
    increment = weigh(localized, selected, scale)
    increment = lax.all_to_all(increment.reshape(senders, 4, cols // 4), "space", 0, 0, tiled=True)
    return increment.reshape(senders, cols)


def solution(mesh):
    return jax.shard_map(
        on_device,
        mesh=mesh,
        in_specs=(
            P("mem", None, "space"),
            P("mem", None, "space"),
            P(),
            P(),
            P(),
            P(),
            P("mem", None),
        ),
        out_specs=P("mem", "space"),
        check_vma=False,
    )
```

```python
import jax
import jax.numpy as jnp
from jax import lax
from jax.experimental import pallas as pl
from jax.experimental.pallas import tpu as pltpu
from jax.sharding import PartitionSpec as P

MIB = 1024 * 1024


def by_level(fields, out_ref):
    owners, own, _, _ = out_ref.shape
    ordered = jnp.swapaxes(fields, 0, 1).astype(jnp.bfloat16)
    for a in range(own):
        out_ref[:, a] = ordered[a * owners : (a + 1) * owners]


def vertical_kernel(loc_ref, alpha_ref, out_ref):
    fields = [
        jnp.dot(loc_ref[...], alpha_ref[m], preferred_element_type=jnp.float32)
        for m in range(alpha_ref.shape[0])
    ]
    by_level(jnp.stack(fields), out_ref)


def vertical(alpha, vertical_loc, owners, steps=2):
    members, levels, cols = alpha.shape
    width = cols // steps
    own = levels // owners
    return pl.pallas_call(
        vertical_kernel,
        grid=(steps,),
        in_specs=[
            pl.BlockSpec((levels, levels), lambda c: (0, 0)),
            pl.BlockSpec((members, levels, width), lambda c: (0, 0, c)),
        ],
        out_specs=pl.BlockSpec((owners, own, members, width), lambda c: (0, 0, 0, c)),
        out_shape=jax.ShapeDtypeStruct((owners, own, members, cols), jnp.bfloat16),
        compiler_params=pltpu.CompilerParams(vmem_limit_bytes=60 * MIB),
        cost_estimate=pl.CostEstimate(
            flops=2 * members * levels * levels * cols,
            bytes_accessed=4 * members * levels * cols,
            transcendentals=0,
        ),
        name="vertical",
    )(vertical_loc, alpha)


def select_kernel(src_ref, pert_ref, out_ref):
    members = pert_ref.shape[0]
    by_level(
        jnp.stack([pert_ref[src_ref[m]].astype(jnp.float32) for m in range(members)]), out_ref
    )


def select(perturbation, member_src, owners, steps=2):
    members, levels, cols = perturbation.shape
    width = cols // steps
    own = levels // owners
    return pl.pallas_call(
        select_kernel,
        grid=(steps,),
        in_specs=[
            pl.BlockSpec(memory_space=pltpu.SMEM),
            pl.BlockSpec((members, levels, width), lambda c: (0, 0, c)),
        ],
        out_specs=pl.BlockSpec((owners, own, members, width), lambda c: (0, 0, 0, c)),
        out_shape=jax.ShapeDtypeStruct((owners, own, members, cols), jnp.bfloat16),
        compiler_params=pltpu.CompilerParams(vmem_limit_bytes=32 * MIB),
        cost_estimate=pl.CostEstimate(
            flops=0, bytes_accessed=4 * members * levels * cols, transcendentals=0
        ),
        name="select",
    )(member_src, perturbation)


def localize_kernel(neigh_ref, slot_ref, vert_ref, blocks_ref, out_ref, slot_of_ref, tiles_ref):
    groups, senders, members, cols = vert_ref.shape
    tile_count, rows, tile = tiles_ref.shape
    nbrs = blocks_ref.shape[0] // tile
    per_sender = cols // tile
    here = out_ref.shape[1]
    block = pl.program_id(0)

    @pl.when(block == 0)
    def _():
        def number(s, carry):
            slot_of_ref[slot_ref[s]] = s
            return carry

        lax.fori_loop(0, tile_count, number, 0, unroll=8)

        def split(sender, carry):
            for g in range(groups):
                for q in range(per_sender):
                    tiles_ref[sender * per_sender + q, g * members : (g + 1) * members] = vert_ref[
                        g, sender, :, q * tile : (q + 1) * tile
                    ]
            return carry

        lax.fori_loop(0, senders, split, 0, unroll=2)

    count = here * per_sender
    firsts = [slot_ref[block * count + i] * nbrs for i in range(count)]

    def picked(i, k):
        return tiles_ref[slot_of_ref[neigh_ref[firsts[i] + k]]]

    total = None
    for k in range(0, nbrs, 2):
        both = range(k, min(k + 2, nbrs))
        left = jnp.concatenate(
            [jnp.concatenate([picked(i, b) for b in both], axis=1) for i in range(count)], axis=0
        )
        term = jnp.dot(
            left,
            blocks_ref[k * tile : (k + len(both)) * tile, :],
            preferred_element_type=jnp.float32,
        )
        total = term if total is None else total + term
    total = total.astype(jnp.bfloat16)
    for i in range(count):
        s, q = divmod(i, per_sender)
        for g in range(groups):
            start = i * rows + g * members
            out_ref[g, s, :, q * tile : (q + 1) * tile] = total[start : start + members]


def localize(vert, neighbours, tile_slot, tile_blocks, here=4):
    groups, senders, members, cols = vert.shape
    rows = groups * members
    nbrs, tile, _ = tile_blocks.shape
    tile_count = tile_slot.shape[0]
    return pl.pallas_call(
        localize_kernel,
        grid=(senders // here,),
        in_specs=[
            pl.BlockSpec(memory_space=pltpu.SMEM),
            pl.BlockSpec(memory_space=pltpu.SMEM),
            pl.BlockSpec((groups, senders, members, cols), lambda b: (0, 0, 0, 0)),
            pl.BlockSpec((nbrs * tile, tile), lambda b: (0, 0)),
        ],
        out_specs=pl.BlockSpec((groups, here, members, cols), lambda b: (0, b, 0, 0)),
        out_shape=jax.ShapeDtypeStruct(vert.shape, jnp.bfloat16),
        input_output_aliases={2: 0},
        scratch_shapes=[
            pltpu.SMEM((tile_count,), jnp.int32),
            pltpu.VMEM((tile_count, rows, tile), jnp.bfloat16),
        ],
        compiler_params=pltpu.CompilerParams(vmem_limit_bytes=24 * MIB),
        cost_estimate=pl.CostEstimate(
            flops=2 * rows * tile_count * nbrs * tile * tile,
            bytes_accessed=4 * rows * tile_count * tile,
            transcendentals=0,
        ),
        name="localize",
    )(neighbours.reshape(-1), tile_slot, vert, tile_blocks.reshape(nbrs * tile, tile))


def weigh_kernel(loc_ref, pert_hbm, out_ref, pert_ref, sems, *, scale):
    parts, groups, here, members, cols = pert_ref.shape
    fetches = [
        pltpu.make_async_copy(pert_hbm.at[:, pl.ds(b * here, here)], pert_ref.at[b], sems.at[b])
        for b in range(parts)
    ]
    for fetch in fetches:
        fetch.start()
    for b in range(parts):
        fetches[b].wait()
        for s in range(here):
            total = jnp.zeros((members, cols), jnp.float32)
            for g in range(groups):
                total = total + loc_ref[g, b * here + s].astype(jnp.float32) * pert_ref[
                    b, g, s
                ].astype(jnp.float32)
            out_ref[b * here + s] = jnp.sum(total, axis=0, keepdims=True) * scale


def weigh(localized, selected, scale, parts=4):
    groups, senders, members, cols = localized.shape
    return pl.pallas_call(
        lambda *refs: weigh_kernel(*refs, scale=scale),
        in_specs=[
            pl.BlockSpec(memory_space=pltpu.VMEM),
            pl.BlockSpec(memory_space=pltpu.HBM),
        ],
        out_specs=pl.BlockSpec(memory_space=pltpu.VMEM),
        out_shape=jax.ShapeDtypeStruct((senders, 1, cols), jnp.float32),
        scratch_shapes=[
            pltpu.VMEM((parts, groups, senders // parts, members, cols), jnp.bfloat16),
            pltpu.SemaphoreType.DMA((parts,)),
        ],
        compiler_params=pltpu.CompilerParams(vmem_limit_bytes=24 * MIB),
        cost_estimate=pl.CostEstimate(
            flops=2 * groups * senders * members * cols,
            bytes_accessed=4 * groups * senders * members * cols,
            transcendentals=0,
        ),
        name="weigh",
    )(localized, selected)


def on_device(alpha, perturbation, vertical_loc, tile_blocks, neighbours, tile_slot, member_src):
    groups, senders = lax.axis_size("mem"), lax.axis_size("space")
    members, levels, cols = alpha.shape
    own = 1
    everyone = ("mem", "space")
    owners = groups * senders
    scale = 1.0 / float(groups * members - 1) ** 0.5

    def to_level_owner(fields):
        fields = lax.all_to_all(fields.reshape(owners, members, cols), everyone, 0, 0, tiled=True)
        return fields.reshape(groups, senders, members, cols)

    vert = to_level_owner(vertical(alpha, vertical_loc, owners))
    selected = to_level_owner(select(perturbation, member_src.reshape(-1), owners))
    localized = localize(vert, neighbours, tile_slot, tile_blocks)
    increment = weigh(localized, selected, scale)
    increment = lax.all_to_all(increment, "space", 0, 0, tiled=True)
    return increment.reshape(senders, cols)


def solution(mesh):
    return jax.shard_map(
        on_device,
        mesh=mesh,
        in_specs=(
            P("mem", None, "space"),
            P("mem", None, "space"),
            P(),
            P(),
            P(),
            P(),
            P("mem", None),
        ),
        out_specs=P("mem", "space"),
        check_vma=False,
    )
```

```python
import jax
import jax.numpy as jnp
from jax import lax
from jax.experimental import pallas as pl
from jax.experimental.pallas import tpu as pltpu
from jax.sharding import PartitionSpec as P

MIB = 1024 * 1024


def by_level(fields, out_ref):
    owners, own, _, _ = out_ref.shape
    ordered = jnp.swapaxes(fields, 0, 1).astype(jnp.bfloat16)
    for a in range(own):
        out_ref[:, a] = ordered[a * owners : (a + 1) * owners]


def vertical_kernel(loc_ref, alpha_ref, out_ref):
    fields = [
        jnp.dot(loc_ref[...], alpha_ref[m], preferred_element_type=jnp.float32)
        for m in range(alpha_ref.shape[0])
    ]
    by_level(jnp.stack(fields), out_ref)


def vertical(alpha, vertical_loc, owners, steps=2):
    members, levels, cols = alpha.shape
    width = cols // steps
    own = levels // owners
    return pl.pallas_call(
        vertical_kernel,
        grid=(steps,),
        in_specs=[
            pl.BlockSpec((levels, levels), lambda c: (0, 0)),
            pl.BlockSpec((members, levels, width), lambda c: (0, 0, c)),
        ],
        out_specs=pl.BlockSpec((owners, own, members, width), lambda c: (0, 0, 0, c)),
        out_shape=jax.ShapeDtypeStruct((owners, own, members, cols), jnp.bfloat16),
        compiler_params=pltpu.CompilerParams(vmem_limit_bytes=60 * MIB),
        cost_estimate=pl.CostEstimate(
            flops=2 * members * levels * levels * cols,
            bytes_accessed=4 * members * levels * cols,
            transcendentals=0,
        ),
        name="vertical",
    )(vertical_loc, alpha)


def select_kernel(src_ref, pert_ref, out_ref):
    members = pert_ref.shape[0]
    by_level(
        jnp.stack([pert_ref[src_ref[m]].astype(jnp.float32) for m in range(members)]), out_ref
    )


def select(perturbation, member_src, owners, steps=2):
    members, levels, cols = perturbation.shape
    width = cols // steps
    own = levels // owners
    return pl.pallas_call(
        select_kernel,
        grid=(steps,),
        in_specs=[
            pl.BlockSpec(memory_space=pltpu.SMEM),
            pl.BlockSpec((members, levels, width), lambda c: (0, 0, c)),
        ],
        out_specs=pl.BlockSpec((owners, own, members, width), lambda c: (0, 0, 0, c)),
        out_shape=jax.ShapeDtypeStruct((owners, own, members, cols), jnp.bfloat16),
        compiler_params=pltpu.CompilerParams(vmem_limit_bytes=32 * MIB),
        cost_estimate=pl.CostEstimate(
            flops=0, bytes_accessed=4 * members * levels * cols, transcendentals=0
        ),
        name="select",
    )(member_src, perturbation)


def localize_kernel(neigh_ref, slot_ref, vert_ref, blocks_ref, out_ref, slot_of_ref, tiles_ref):
    groups, senders, members, cols = vert_ref.shape
    tile_count, rows, tile = tiles_ref.shape
    nbrs = blocks_ref.shape[0] // tile
    per_sender = cols // tile
    here = out_ref.shape[1]
    block = pl.program_id(0)

    @pl.when(block == 0)
    def _():
        def number(s, carry):
            slot_of_ref[slot_ref[s]] = s
            return carry

        lax.fori_loop(0, tile_count, number, 0, unroll=8)

        def split(sender, carry):
            for g in range(groups):
                for q in range(per_sender):
                    tiles_ref[sender * per_sender + q, g * members : (g + 1) * members] = vert_ref[
                        g, sender, :, q * tile : (q + 1) * tile
                    ]
            return carry

        lax.fori_loop(0, senders, split, 0, unroll=2)

    count = here * per_sender
    firsts = [slot_ref[block * count + i] * nbrs for i in range(count)]

    def picked(i, k):
        return tiles_ref[slot_of_ref[neigh_ref[firsts[i] + k]]]

    total = None
    for k in range(0, nbrs, 2):
        both = range(k, min(k + 2, nbrs))
        left = jnp.concatenate(
            [jnp.concatenate([picked(i, b) for b in both], axis=1) for i in range(count)], axis=0
        )
        term = jnp.dot(
            left,
            blocks_ref[k * tile : (k + len(both)) * tile, :],
            preferred_element_type=jnp.float32,
        )
        total = term if total is None else total + term
    total = total.astype(jnp.bfloat16)
    for i in range(count):
        s, q = divmod(i, per_sender)
        for g in range(groups):
            start = i * rows + g * members
            out_ref[g, s, :, q * tile : (q + 1) * tile] = total[start : start + members]


def localize(vert, neighbours, tile_slot, tile_blocks, here=4):
    groups, senders, members, cols = vert.shape
    rows = groups * members
    nbrs, tile, _ = tile_blocks.shape
    tile_count = tile_slot.shape[0]
    return pl.pallas_call(
        localize_kernel,
        grid=(senders // here,),
        in_specs=[
            pl.BlockSpec(memory_space=pltpu.SMEM),
            pl.BlockSpec(memory_space=pltpu.SMEM),
            pl.BlockSpec((groups, senders, members, cols), lambda b: (0, 0, 0, 0)),
            pl.BlockSpec((nbrs * tile, tile), lambda b: (0, 0)),
        ],
        out_specs=pl.BlockSpec((groups, here, members, cols), lambda b: (0, b, 0, 0)),
        out_shape=jax.ShapeDtypeStruct(vert.shape, jnp.bfloat16),
        input_output_aliases={2: 0},
        scratch_shapes=[
            pltpu.SMEM((tile_count,), jnp.int32),
            pltpu.VMEM((tile_count, rows, tile), jnp.bfloat16),
        ],
        compiler_params=pltpu.CompilerParams(vmem_limit_bytes=24 * MIB),
        cost_estimate=pl.CostEstimate(
            flops=2 * rows * tile_count * nbrs * tile * tile,
            bytes_accessed=4 * rows * tile_count * tile,
            transcendentals=0,
        ),
        name="localize",
    )(neighbours.reshape(-1), tile_slot, vert, tile_blocks.reshape(nbrs * tile, tile))


def weigh_kernel(loc_ref, pert_hbm, out_ref, pert_ref, sems, *, scale):
    parts, groups, here, members, cols = pert_ref.shape
    fetches = [
        pltpu.make_async_copy(pert_hbm.at[:, pl.ds(b * here, here)], pert_ref.at[b], sems.at[b])
        for b in range(parts)
    ]
    for fetch in fetches:
        fetch.start()
    for b in range(parts):
        fetches[b].wait()
        for s in range(here):
            total = jnp.zeros((members, cols), jnp.float32)
            for g in range(groups):
                total = total + loc_ref[g, b * here + s].astype(jnp.float32) * pert_ref[
                    b, g, s
                ].astype(jnp.float32)
            out_ref[b * here + s] = jnp.sum(total, axis=0, keepdims=True) * scale


def weigh(localized, selected, scale, parts=8):
    groups, senders, members, cols = localized.shape
    return pl.pallas_call(
        lambda *refs: weigh_kernel(*refs, scale=scale),
        in_specs=[
            pl.BlockSpec(memory_space=pltpu.VMEM),
            pl.BlockSpec(memory_space=pltpu.HBM),
        ],
        out_specs=pl.BlockSpec(memory_space=pltpu.VMEM),
        out_shape=jax.ShapeDtypeStruct((senders, 1, cols), jnp.float32),
        scratch_shapes=[
            pltpu.VMEM((parts, groups, senders // parts, members, cols), jnp.bfloat16),
            pltpu.SemaphoreType.DMA((parts,)),
        ],
        compiler_params=pltpu.CompilerParams(vmem_limit_bytes=24 * MIB),
        cost_estimate=pl.CostEstimate(
            flops=2 * groups * senders * members * cols,
            bytes_accessed=4 * groups * senders * members * cols,
            transcendentals=0,
        ),
        name="weigh",
    )(localized, selected)


def on_device(alpha, perturbation, vertical_loc, tile_blocks, neighbours, tile_slot, member_src):
    groups, senders = lax.axis_size("mem"), lax.axis_size("space")
    members, levels, cols = alpha.shape
    own = 1
    everyone = ("mem", "space")
    owners = groups * senders
    scale = 1.0 / float(groups * members - 1) ** 0.5

    def to_level_owner(fields):
        fields = lax.all_to_all(fields.reshape(owners, members, cols), everyone, 0, 0, tiled=True)
        return fields.reshape(groups, senders, members, cols)

    vert = to_level_owner(vertical(alpha, vertical_loc, owners))
    selected = to_level_owner(select(perturbation, member_src.reshape(-1), owners))
    localized = localize(vert, neighbours, tile_slot, tile_blocks)
    increment = weigh(localized, selected, scale)
    increment = lax.all_to_all(increment, "space", 0, 0, tiled=True)
    return increment.reshape(senders, cols)


def solution(mesh):
    return jax.shard_map(
        on_device,
        mesh=mesh,
        in_specs=(
            P("mem", None, "space"),
            P("mem", None, "space"),
            P(),
            P(),
            P(),
            P(),
            P("mem", None),
        ),
        out_specs=P("mem", "space"),
        check_vma=False,
    )
```
